512 devices in a mesh: member: 8 (over z_hi, core), grid: 64 (over y, z_lo, x).
Axes of the slice: x: 4, y: 4, z: 16 (z_hi: 4, z_lo: 4; z = z_hi * 4 + z_lo), core: 2. Of those that a mesh axis runs over, the one named last changes fastest.
Arguments:
- node_feats: bfloat16 [8, 32768, 1024], P('member', 'grid'), may hold values from -6 to 6
- norm_gain: bfloat16 [1024], replicated, may hold values from 0.099609375 to 1.8984375
- w_query: bfloat16 [1024, 1024], P('grid'), may hold values from -0.1875 to 0.1875
- w_key: bfloat16 [1024, 1024], P('grid'), may hold values from -0.1875 to 0.1875
- w_value: bfloat16 [1024, 1024], P('grid'), may hold values from -0.1875 to 0.1875
- w_out: bfloat16 [1024, 1024], P('grid'), may hold values from -0.1875 to 0.1875
- head_scale: float32 [16], replicated, may hold values from 2 to 600
- w_dec: bfloat16 [100, 1024], replicated, may hold values from -0.1875 to 0.1875
- targets: bfloat16 [100, 65536], P(None, 'grid'), may hold values from -6 to 6
- cell_node: int32 [65536], P('grid'), may hold values from 0 to 511
- cell_area: float32 [65536], P('grid'), may hold values from 0.002 to 0.02
Outputs:
- member_score: float32 [8, 100, 65536], P('member', None, 'grid')
- grad_dec: float32 [100, 1024], replicated
The draws below stay inside these ranges and needn't reach their ends.
All inputs are finite; a program needn't handle non-finite values.
Results may differ from the reference program's by a relative error of at most 0.0095.
The reference program's roundings to bfloat16 on the way (of `normed`, `query`, `weights`, `attended`, `hidden`, `fields` and `node_grad`) count: a program that leaves them out, or rounds other values in their place, can miss the bound.
Values may be sent and summed in bfloat16 or wider, within the bound.
No kernel may reach another device: no remote copies, remote signals or barrier semaphores. Data moves between devices by JAX's collectives and lax.ppermute only.
A program may use at most 64 MiB of HBM per device.

```python
import math
import jax
import jax.numpy as jnp
from jax import lax

D = 1024
HEADS = 16
VARS = 100
WIN = 512
NODE_DEV = 512
CELL_DEV = 1024
MEMBERS = 8
NODES = 32768
CELLS = 65536


def draw_head_scale(key, part):
    key = jax.random.fold_in(key, 7)
    low, high = (math.log(2.0), math.log(12.0))
    uniform_draw = jax.random.uniform(key, (HEADS,), jnp.float32)
    return jnp.exp(low + (high - low) * uniform_draw)


def with_ends(drawn, stream_key, least, high):
    longest = drawn.shape.index(max(drawn.shape))
    spots = []
    for shift in (0, 1):
        where = [jax.random.randint(jax.random.fold_in(stream_key, axis), (), 0, length) for axis, length in enumerate(drawn.shape)]
        where[longest] = (where[longest] + shift) % drawn.shape[longest]
        spots.append(tuple(where))
    return drawn.at[spots[0]].set(least).at[spots[1]].set(high)


def shard_levels(key, dims, split, low, high):
    loudness, own = 1.0, jax.random.fold_in(key, 6)
    for position, shards_of in split:
        heights = jnp.exp(jax.random.uniform(jax.random.fold_in(own, position), (shards_of,), jnp.float32, low / len(split), high / len(split)))
        loudness = loudness * jnp.repeat(heights, dims[position] // shards_of).reshape([-1 if axis == position else 1 for axis in range(len(dims))])
    return loudness


def noise(rng, dims, scale, limit, shards=(), held_as=jnp.bfloat16):
    array = scale * jax.random.normal(rng, dims, jnp.float32)
    if shards:
        array = array * shard_levels(rng, dims, shards, -0.22, 0.18)
    return jnp.clip(array, -limit, limit).astype(held_as)


def setup_inputs(seed: int = 0) -> dict:
    key_of = jax.random.split(jax.random.key(seed), 12)
    node_feats = noise(key_of[0], (MEMBERS, NODES, D), 1.0, 6.0, ((0, 8), (1, 64)))
    norm_gain = jnp.clip(1.0 + 0.18 * jax.random.normal(key_of[1], (D,), jnp.float32), 0.099609375, 1.8984375).astype(jnp.bfloat16)
    w_query = noise(key_of[2], (D, D), D ** -0.5, 0.1875, ((0, 64),))
    w_key = noise(key_of[3], (D, D), D ** -0.5, 0.1875, ((0, 64),))
    w_value = noise(key_of[4], (D, D), D ** -0.5, 0.1875, ((0, 64),))
    w_out = noise(key_of[5], (D, D), D ** -0.5, 0.1875, ((0, 64),))
    head_scale = draw_head_scale(jax.random.fold_in(key_of[11], 71), 0)
    w_dec = noise(key_of[7], (VARS, D), D ** -0.5, 0.1875)
    targets = noise(key_of[8], (VARS, CELLS), 1.0, 6.0, ((1, 64),))
    cell_node = with_ends(jax.random.randint(key_of[9], (CELLS,), 0, NODE_DEV), jax.random.fold_in(key_of[9], 1), 0, NODE_DEV - 1).astype(jnp.int32)
    cell_area = jnp.clip(jnp.exp(math.log(0.02) - 2.30258502 * jax.random.uniform(key_of[10], (CELLS,), jnp.float32) ** shard_levels(key_of[10], (CELLS,), ((0, 64),), -0.2, 0.2)), 0.002, 0.02)
    return dict(node_feats=node_feats, norm_gain=norm_gain, w_query=w_query, w_key=w_key, w_value=w_value, w_out=w_out, head_scale=head_scale, w_dec=w_dec, targets=targets, cell_node=cell_node, cell_area=cell_area)


EPS = 1e-06
SMOOTH_SQ = 0.0625
ALPHA = 0.95

def rms_norm(features, gain):
    values = features.astype(jnp.float32)
    scale = lax.rsqrt(lax.optimization_barrier(jnp.mean(values * values, -1, keepdims=True)) + EPS)
    return (values * scale * gain.astype(jnp.float32)).astype(jnp.bfloat16)

def unit_rows(tensor):
    return tensor * lax.rsqrt(lax.optimization_barrier(jnp.sum(tensor * tensor, -1, keepdims=True)) + EPS)

def member_forward(features, norm_gain, w_query, w_key, w_value, w_out, head_scale, w_dec, node_index):
    heads = head_scale.shape[0]
    head_dim = D // heads
    half = WIN // 2
    normed = rms_norm(features, norm_gain)
    query = jnp.dot(normed, w_query, preferred_element_type=jnp.float32).reshape(NODES, heads, head_dim)
    query = (unit_rows(query) * head_scale[None, :, None]).astype(jnp.bfloat16)
    keys = jnp.dot(normed, w_key, preferred_element_type=jnp.float32).reshape(NODES, heads, head_dim)
    keys = unit_rows(keys).astype(jnp.bfloat16)
    values = jnp.dot(normed, w_value, preferred_element_type=jnp.float32).astype(jnp.bfloat16)
    values = values.reshape(NODES, heads, head_dim)
    keys_pad = jnp.pad(keys, ((half, half), (0, 0), (0, 0)))
    values_pad = jnp.pad(values, ((half, half), (0, 0), (0, 0)))

    def block(index):
        start = index * NODE_DEV
        query_blk = lax.dynamic_slice_in_dim(query, start, NODE_DEV, 0)
        keys_blk = lax.dynamic_slice_in_dim(keys_pad, start, NODE_DEV + 2 * half, 0)
        values_blk = lax.dynamic_slice_in_dim(values_pad, start, NODE_DEV + 2 * half, 0)
        query_pos = start + jnp.arange(NODE_DEV, dtype=jnp.int32)
        key_pos = start - half + jnp.arange(NODE_DEV + 2 * half, dtype=jnp.int32)
        offset = key_pos[None, :] - query_pos[:, None]
        allowed = (offset >= -half) & (offset < half) & (key_pos >= 0)[None, :] & (key_pos < NODES)[None, :]
        score = jnp.einsum('nhd,ehd->hne', query_blk.astype(jnp.float32), keys_blk.astype(jnp.float32))
        score = jnp.where(allowed[None], score, -jnp.inf)
        top = lax.optimization_barrier(jnp.max(score, -1, keepdims=True))
        expo = jnp.exp(score - top)
        weights = (expo / lax.optimization_barrier(jnp.sum(expo, -1, keepdims=True))).astype(jnp.bfloat16)
        mixed = jnp.einsum('hne,ehd->nhd', weights.astype(jnp.float32), values_blk.astype(jnp.float32))
        return mixed.reshape(NODE_DEV, D).astype(jnp.bfloat16)
    attended = lax.map(block, jnp.arange(NODES // NODE_DEV, dtype=jnp.int32)).reshape(NODES, D)
    hidden = (features.astype(jnp.float32) + jnp.dot(attended, w_out, preferred_element_type=jnp.float32)).astype(jnp.bfloat16)
    node_out = jnp.dot(w_dec, hidden.T, preferred_element_type=jnp.float32)
    fields = jnp.take(node_out, node_index, axis=1).astype(jnp.bfloat16)
    return (hidden, fields)

def reference(node_feats, norm_gain, w_query, w_key, w_value, w_out, head_scale, w_dec, targets, cell_node, cell_area):
    node_index = jnp.arange(CELLS, dtype=jnp.int32) // CELL_DEV * NODE_DEV + cell_node.astype(jnp.int32)

    def run(features):
        return member_forward(features, norm_gain, w_query, w_key, w_value, w_out, head_scale, w_dec, node_index)
    hidden_all, fields_all = lax.map(run, node_feats)
    fields_f = fields_all.astype(jnp.float32)
    truth = targets.astype(jnp.float32)
    kappa = ALPHA / (2.0 * MEMBERS * (MEMBERS - 1)) + (1.0 - ALPHA) / (2.0 * MEMBERS * MEMBERS)
    scores = []
    grad_dec = jnp.zeros((VARS, D), jnp.float32)
    for member in range(MEMBERS):
        own = fields_f[member]
        spread = jnp.zeros_like(own)
        slope = jnp.zeros_like(own)
        for other in range(MEMBERS):
            if other != member:
                delta = own - fields_f[other]
                smooth = jnp.sqrt(delta * delta + SMOOTH_SQ)
                spread = spread + smooth
                slope = slope + delta / smooth
        error = own - truth
        error_s = jnp.sqrt(error * error + SMOOTH_SQ)
        scores.append(error_s / MEMBERS - kappa * spread)
        cell_grad = cell_area[None, :] * (error / error_s / MEMBERS - 2.0 * kappa * slope)
        node_grad = jax.ops.segment_sum(cell_grad.T, node_index, NODES).T.astype(jnp.bfloat16)
        grad_dec = grad_dec + jnp.dot(node_grad, hidden_all[member], preferred_element_type=jnp.float32)
    return (jnp.stack(scores, 0), grad_dec)
```

```python
import functools

import jax
import jax.numpy as jnp
from jax import lax
from jax.experimental import pallas as pl
from jax.experimental.pallas import tpu as pltpu
from jax.sharding import Mesh, PartitionSpec as P

HALF = 256
EPS = 1e-06
SMOOTH_SQ = 0.0625
ALPHA = 0.95
LANES = 128
BLOCK = 128
LOW = -1e30
MIB = 1024 * 1024

GRID = ("y", "z_lo", "x")
MEMBER = ("z_hi", "core")

f32 = jnp.float32
bf16 = jnp.bfloat16


def dot(a, b):
    return jnp.dot(a, b, preferred_element_type=f32)


def dot_t(a, b):
    return lax.dot_general(a, b, (((1,), (1,)), ((), ())), preferred_element_type=f32)


def halves(x):
    high = x.astype(bf16)
    return high, (x - high.astype(f32)).astype(bf16)


def loop(count, fn):
    def step(i, _):
        fn(i)
        return 0

    lax.fori_loop(0, count, step, 0)


def normalise(before, feats, after, gain, normed):
    gain_row = gain[...].astype(f32)
    start = 0
    for ref in (before, feats, after):

        def norm(i, ref=ref, start=start):
            x = ref[pl.ds(pl.multiple_of(i * 64, 64), 64), :].astype(f32)
            mean = jnp.mean(x * x, -1, keepdims=True)
            y = x * lax.rsqrt(mean + EPS) * gain_row
            normed[pl.ds(pl.multiple_of(start + i * 64, 64), 64), :] = y.astype(bf16)

        loop(ref.shape[0] // 64, norm)
        start += ref.shape[0]


def weight_copies(gathered_weights, weights, sems):
    ys, xs, zs, rows, _ = gathered_weights.shape
    copies = []
    for y in range(ys):
        for z in range(zs):
            copies.append(
                pltpu.make_async_copy(
                    gathered_weights.at[y, :, z], weights.at[y * zs + z], sems.at[y * zs + z]
                )
            )
    return copies


def attend_half(edge, normed, weights, scale, query, keys, values, put):
    ext, width = normed.shape
    nodes = ext - 2 * HALF
    mine = scale.shape[1]
    heads_of = lambda axis: lax.broadcasted_iota(jnp.int32, (256, 256), axis) // 64
    same_head = (heads_of(0) == heads_of(1)).astype(bf16)

    def unit(y):
        high, low = halves(y * y)
        total = dot(high, same_head) + dot(low, same_head)
        return y * lax.rsqrt(total + EPS)

    flat = weights.reshape(width, weights.shape[-1])

    def project(c):
        start = pl.multiple_of(c * 256, 256)
        cols = pl.ds(start, 256)
        key_cols = pl.ds(pl.multiple_of(mine + start, 256), 256)
        value_cols = pl.ds(pl.multiple_of(2 * mine + start, 256), 256)
        for r in range(nodes // 256):
            rows = pl.ds(r * 256, 256)
            y = dot(normed[pl.ds(HALF + r * 256, 256), :], flat[:, cols])
            query[rows, cols] = (unit(y) * scale[:, cols]).astype(bf16)
        for r in range(ext // 256):
            rows = pl.ds(r * 256, 256)
            keys[rows, cols] = unit(dot(normed[rows, :], flat[:, key_cols])).astype(bf16)
            values[rows, cols] = dot(normed[rows, :], flat[:, value_cols]).astype(bf16)

    loop(mine // 256, project)

    row = lax.broadcasted_iota(jnp.int32, (2 * BLOCK, BLOCK), 0) % BLOCK
    col = lax.broadcasted_iota(jnp.int32, (2 * BLOCK, BLOCK), 1)
    lead = jnp.where(col >= row, 0.0, LOW).astype(f32)
    tail = jnp.where(col < row, 0.0, LOW).astype(f32)
    first_head = lax.broadcasted_iota(jnp.int32, (BLOCK, LANES), 1) < 64
    ones = jnp.ones((2 * HALF + BLOCK, LANES), bf16)
    segments = 2 * HALF // BLOCK + 1
    blocks = nodes // BLOCK
    out_low = jnp.where(edge[0] == 0, LOW, 0.0).astype(f32)
    out_high = jnp.where(edge[0] == edge[1] - 1, LOW, 0.0).astype(f32)

    def attend(p):
        cols = pl.ds(pl.multiple_of(p * LANES, LANES), LANES)
        for b in range(blocks):
            rows = pl.ds(b * BLOCK, BLOCK)
            window = pl.ds(b * BLOCK, 2 * HALF + BLOCK)
            q = query[rows, cols]
            zero = jnp.zeros_like(q)
            pair = jnp.concatenate([jnp.where(first_head, q, zero), jnp.where(first_head, zero, q)], 0)
            score = dot_t(pair, keys[window, cols])
            parts = []
            for s in range(segments):
                part = score[:, s * BLOCK : (s + 1) * BLOCK]
                if s == 0:
                    part = part + lead
                if s == segments - 1:
                    part = part + tail
                if (b + s + 1) * BLOCK <= HALF:
                    part = part + out_low
                if (b + s) * BLOCK >= HALF + nodes:
                    part = part + out_high
                parts.append(part)
            top = functools.reduce(jnp.maximum, parts)
            top = jnp.max(top, -1, keepdims=True)
            weight = jnp.concatenate([jnp.exp(part - top).astype(bf16) for part in parts], 1)
            mixed = dot(weight, jnp.concatenate([values[window, cols], ones], 1))
            mixed = mixed[:, :LANES] / mixed[:, LANES:]
            put(rows, cols, jnp.where(first_head, mixed[:BLOCK], mixed[BLOCK:]).astype(bf16))

    loop(mine // LANES, attend)


def first_kernel(
    edge, before, feats, after, gain, gathered_weights, scale,
    attended, normed,
    weights, query, keys, values, sems,
):
    mine = scale.shape[1]
    copies = weight_copies(gathered_weights.at[..., pl.ds(0, 3 * mine)], weights, sems)
    for copy in copies:
        copy.start()
    normalise(before, feats, after, gain, normed)
    for copy in copies:
        copy.wait()

    def put(rows, cols, value):
        attended[rows, cols] = value

    attend_half(edge, normed, weights, scale, query, keys, values, put)


def second_kernel(
    edge, feats, normed, gathered_mine, gathered_other, scale, attended_mine, w_dec,
    hidden_out, fields_out,
    weights, out_mine, out_other, query, keys, values, attended, sems, sems_mine, sems_other,
):
    nodes, width = feats.shape
    mine = scale.shape[1]
    copies = weight_copies(gathered_other.at[..., pl.ds(0, 3 * mine)], weights, sems)
    copies_out = weight_copies(gathered_mine.at[..., pl.ds(3 * mine, mine)], out_mine, sems_mine)
    copies_out += weight_copies(gathered_other.at[..., pl.ds(3 * mine, mine)], out_other, sems_other)
    for copy in copies + copies_out:
        copy.start()
    here = pl.multiple_of(edge[2] * mine, mine)
    there = pl.multiple_of((1 - edge[2]) * mine, mine)
    attended[:, pl.ds(here, mine)] = attended_mine[...]
    for copy in copies:
        copy.wait()

    def put(rows, cols, value):
        attended[rows, pl.ds(pl.multiple_of(there + cols.start, LANES), LANES)] = value

    attend_half(edge, normed, weights, scale, query, keys, values, put)
    for copy in copies_out:
        copy.wait()
    for half, start in ((out_mine, here), (out_other, there)):
        flat = half.reshape(width, mine)

        def finish(r, flat=flat, start=start):
            rows = pl.ds(pl.multiple_of(r * 256, 256), 256)
            cols = pl.ds(start, mine)
            hidden = feats[rows, cols].astype(f32) + dot(attended[rows, :], flat[...])
            hidden_out[rows, cols] = hidden.astype(bf16)

        loop(nodes // 256, finish)
    fields_out[...] = dot_t(w_dec[...], hidden_out[...]).astype(bf16)


def score_kernel(
    own, same_core, other_core, hidden, targets, cell_node, cell_area,
    score_out, grad_out,
):
    members = 2 * same_core.shape[0]
    nodes = own.shape[1]
    variables, cells = targets.shape
    mine = own[...].astype(f32)
    spread = jnp.zeros_like(mine) - SMOOTH_SQ**0.5
    slope = jnp.zeros_like(mine)
    for ref in (same_core, other_core):
        for j in range(members // 2):
            delta = mine - ref[j].astype(f32)
            square = delta * delta + SMOOTH_SQ
            inverse = lax.rsqrt(square)
            spread = spread + square * inverse
            slope = slope + delta * inverse
    kappa = ALPHA / (2.0 * members * (members - 1)) + (1.0 - ALPHA) / (2.0 * members * members)
    index = lax.broadcasted_iota(jnp.int32, (nodes, cells), 0)
    one_hot = (index == cell_node[...]).astype(bf16)
    high, low = halves(spread)
    fields = dot(own[...], one_hot)
    spread = dot(high, one_hot) + dot(low, one_hot)
    error = fields - targets[...].astype(f32)
    square = error * error + SMOOTH_SQ
    inverse = lax.rsqrt(square)
    score_out[...] = square * inverse * (1.0 / members) - kappa * spread
    area = cell_area[...]
    high, low = halves(area * (error * inverse) * (1.0 / members))
    area_high, area_low = halves(jnp.broadcast_to(area, (8, cells)))
    node_grad = dot_t(high, one_hot) + dot_t(low, one_hot)
    node_area = dot_t(area_high, one_hot) + dot_t(area_low, one_hot)
    node_grad = node_grad - (2.0 * kappa) * slope * node_area[:1]
    grad = dot(node_grad.astype(bf16), hidden[...])
    tiles = grad.shape[1] // LANES
    grad = jnp.concatenate([grad, jnp.zeros((128 - variables, grad.shape[1]), f32)], 0)
    for r in range(128 // 8):
        for c in range(tiles):
            tile = r * tiles + c
            grad_out[tile // 2, pl.ds(tile % 2 * 8, 8), :] = grad[r * 8 : r * 8 + 8, c * LANES : (c + 1) * LANES]


def shifted(value, axis, steps):
    count = lax.axis_size(axis)
    return lax.ppermute(value, axis, [(i, (i + steps) % count) for i in range(count)])


def gathered(x, axis):
    count = lax.axis_size(axis)
    return lax.all_to_all(jnp.broadcast_to(x[None], (count,) + x.shape), axis, 0, 0)


def total(pieces):
    piece = jnp.sum(lax.all_to_all(pieces, GRID, 0, 0), 0)
    piece = jnp.sum(gathered(piece, MEMBER), 0)
    return gathered(piece, GRID)


def body(
    node_feats, norm_gain, w_query, w_key, w_value, w_out, head_scale, w_dec, targets, cell_node, cell_area
):
    feats = node_feats[0]
    nodes, width = feats.shape
    ext = nodes + 2 * HALF
    shards = lax.axis_size(GRID)
    core = lax.axis_index("core")
    variables = w_dec.shape[0]
    up = [(i, i + 1) for i in range(shards - 1)]
    before = lax.ppermute(feats[nodes - HALF :], GRID, up)
    after = lax.ppermute(feats[:HALF], GRID, [(j, i) for i, j in up])

    mine = width // 2
    parts = [
        lax.dynamic_slice_in_dim(w, core * mine, mine, 1) for w in (w_query, w_key, w_value, w_out)
    ]
    shard = jnp.concatenate(parts, 1)
    rows, columns = shard.shape
    lines = lax.axis_size("z_lo")
    lane = gathered(shard, "z_lo")
    whole = gathered(lane, ("y", "x"))
    whole = whole.reshape(lax.axis_size("y"), lax.axis_size("x"), lines, rows, columns)
    other = shifted(whole, "core", 1)

    scale = jnp.repeat(head_scale, width // head_scale.shape[0])[None]
    scale_mine = lax.dynamic_slice_in_dim(scale, core * mine, mine, 1)
    scale_other = lax.dynamic_slice_in_dim(scale, (1 - core) * mine, mine, 1)
    edge = jnp.stack([lax.axis_index(GRID), jnp.int32(shards), core]).astype(jnp.int32)
    smem = pl.BlockSpec(memory_space=pltpu.SMEM)
    vmem = pl.BlockSpec(memory_space=pltpu.VMEM)
    anywhere = pl.BlockSpec(memory_space=pl.ANY)
    params = pltpu.CompilerParams(vmem_limit_bytes=48 * MIB)
    groups = shards // lax.axis_size("x")
    weights = lambda n: pltpu.VMEM((groups, shards // groups, rows, n), bf16)
    heads = [pltpu.VMEM((n, mine), bf16) for n in (nodes, ext, ext)]
    attended, normed = pl.pallas_call(
        first_kernel,
        out_shape=(
            jax.ShapeDtypeStruct((nodes, mine), bf16),
            jax.ShapeDtypeStruct((ext, width), bf16),
        ),
        in_specs=[smem] + [vmem] * 4 + [anywhere, vmem],
        out_specs=(vmem, vmem),
        scratch_shapes=[weights(3 * mine), *heads, pltpu.SemaphoreType.DMA((groups,))],
        compiler_params=params,
        cost_estimate=pl.CostEstimate(flops=8_000_000_000, bytes_accessed=8_000_000, transcendentals=0),
        name="first_heads",
    )(edge, before, feats, after, norm_gain[None], whole, scale_mine)
    hidden, fields = pl.pallas_call(
        second_kernel,
        out_shape=(
            jax.ShapeDtypeStruct((nodes, width), bf16),
            jax.ShapeDtypeStruct((variables, nodes), bf16),
        ),
        in_specs=[smem, vmem, vmem, anywhere, anywhere, vmem, vmem, vmem],
        out_specs=(vmem, vmem),
        scratch_shapes=[
            weights(3 * mine),
            weights(mine),
            weights(mine),
            *heads,
            pltpu.VMEM((nodes, width), bf16),
            pltpu.SemaphoreType.DMA((groups,)),
            pltpu.SemaphoreType.DMA((groups,)),
            pltpu.SemaphoreType.DMA((groups,)),
        ],
        compiler_params=params,
        name="second_heads",
    )(edge, feats, normed, whole, other, scale_other, attended, w_dec)

    same_core = gathered(fields, "z_hi")
    other_core = shifted(same_core, "core", 1)
    score, pieces = pl.pallas_call(
        score_kernel,
        out_shape=(
            jax.ShapeDtypeStruct(targets.shape, f32),
            jax.ShapeDtypeStruct((shards, 16, LANES), f32),
        ),
        in_specs=[vmem] * 7,
        out_specs=(vmem, vmem),
        compiler_params=params,
        name="score",
    )(fields, same_core, other_core, hidden, targets, cell_node[None], cell_area[None])
    grad = total(pieces).reshape(16, width // LANES, 8, LANES).transpose(0, 2, 1, 3)
    return score[None], grad.reshape(128, width)[:variables]


def solution(mesh):
    fine = Mesh(mesh.devices.reshape(4, 2, 4, 4, 4), MEMBER + GRID)
    in_specs = (
        P(MEMBER, GRID, None),
        P(),
        P(GRID, None),
        P(GRID, None),
        P(GRID, None),
        P(GRID, None),
        P(),
        P(),
        P(None, GRID),
        P(GRID),
        P(GRID),
    )
    out_specs = (P(MEMBER, None, GRID), P())
    return jax.shard_map(body, mesh=fine, in_specs=in_specs, out_specs=out_specs, check_vma=False)
```

```python
import functools

import jax
import jax.numpy as jnp
from jax import lax
from jax.experimental import pallas as pl
from jax.experimental.pallas import tpu as pltpu
from jax.sharding import Mesh, PartitionSpec as P

HALF = 256
EPS = 1e-06
SMOOTH_SQ = 0.0625
ALPHA = 0.95
LANES = 128
BLOCK = 128
LOW = -1e30
MIB = 1024 * 1024

GRID = ("y", "z_lo", "x")
MEMBER = ("z_hi", "core")
PLANE = ("core", "y", "x")
LINE = ("z_hi", "z_lo")

f32 = jnp.float32
bf16 = jnp.bfloat16


def dot(a, b):
    return jnp.dot(a, b, preferred_element_type=f32)


def dot_t(a, b):
    return lax.dot_general(a, b, (((1,), (1,)), ((), ())), preferred_element_type=f32)


def halves(x):
    high = x.astype(bf16)
    return high, (x - high.astype(f32)).astype(bf16)


def loop(count, fn):
    def step(i, _):
        fn(i)
        return 0

    lax.fori_loop(0, count, step, 0)


def normalise(before, feats, after, gain, normed):
    gain_row = gain[...].astype(f32)
    start = 0
    for ref in (before, feats, after):

        def norm(i, ref=ref, start=start):
            x = ref[pl.ds(pl.multiple_of(i * 64, 64), 64), :].astype(f32)
            mean = jnp.mean(x * x, -1, keepdims=True)
            y = x * lax.rsqrt(mean + EPS) * gain_row
            normed[pl.ds(pl.multiple_of(start + i * 64, 64), 64), :] = y.astype(bf16)

        loop(ref.shape[0] // 64, norm)
        start += ref.shape[0]


def weight_copies(gathered_weights, weights, sems):
    ys, xs, zs, rows, _ = gathered_weights.shape
    copies = []
    for y in range(ys):
        for z in range(zs):
            copies.append(
                pltpu.make_async_copy(
                    gathered_weights.at[y, :, z], weights.at[y * zs + z], sems.at[y * zs + z]
                )
            )
    return copies


def attend_pairs(edge, normed, weights, scale, base, query, keys, values, attended):
    ext, width = normed.shape
    nodes = ext - 2 * HALF
    pairs = weights.shape[-1] // (3 * LANES)
    flat = weights.reshape(width, weights.shape[-1])

    def unit(y):
        first_head = lax.broadcasted_iota(jnp.int32, y.shape, 1) < 64
        square = y * y
        first = jnp.sum(jnp.where(first_head, square, 0.0), -1, keepdims=True)
        second = jnp.sum(jnp.where(first_head, 0.0, square), -1, keepdims=True)
        return y * lax.rsqrt(jnp.where(first_head, first, second) + EPS)

    for p in range(pairs):
        cols = pl.ds(p * LANES, LANES)
        query_cols = pl.ds(p * 3 * LANES, LANES)
        keyval_cols = pl.ds(p * 3 * LANES + LANES, 2 * LANES)
        factor = scale[:, pl.ds(pl.multiple_of(base + p * LANES, LANES), LANES)]
        for r in range(nodes // 256):
            rows = pl.ds(r * 256, 256)
            y = dot(normed[pl.ds(HALF + r * 256, 256), :], flat[:, query_cols])
            query[rows, cols] = (unit(y) * factor).astype(bf16)
        for r in range(ext // 256):
            rows = pl.ds(r * 256, 256)
            y = dot(normed[rows, :], flat[:, keyval_cols])
            keys[rows, cols] = unit(y[:, :LANES]).astype(bf16)
            values[rows, cols] = y[:, LANES:].astype(bf16)

    row = lax.broadcasted_iota(jnp.int32, (2 * BLOCK, BLOCK), 0) % BLOCK
    col = lax.broadcasted_iota(jnp.int32, (2 * BLOCK, BLOCK), 1)
    lead = jnp.where(col >= row, 0.0, LOW).astype(f32)
    tail = jnp.where(col < row, 0.0, LOW).astype(f32)
    first_head = lax.broadcasted_iota(jnp.int32, (BLOCK, LANES), 1) < 64
    ones = jnp.ones((2 * HALF + BLOCK, LANES), bf16)
    segments = 2 * HALF // BLOCK + 1
    out_low = jnp.where(edge[0] == 0, LOW, 0.0).astype(f32)
    out_high = jnp.where(edge[0] == edge[1] - 1, LOW, 0.0).astype(f32)
    for p in range(pairs):
        cols = pl.ds(p * LANES, LANES)
        for b in range(nodes // BLOCK):
            rows = pl.ds(b * BLOCK, BLOCK)
            window = pl.ds(b * BLOCK, 2 * HALF + BLOCK)
            q = query[rows, cols]
            zero = jnp.zeros_like(q)
            pair = jnp.concatenate([jnp.where(first_head, q, zero), jnp.where(first_head, zero, q)], 0)
            score = dot_t(pair, keys[window, cols])
            parts = []
            for s in range(segments):
                part = score[:, s * BLOCK : (s + 1) * BLOCK]
                if s == 0:
                    part = part + lead
                if s == segments - 1:
                    part = part + tail
                if (b + s + 1) * BLOCK <= HALF:
                    part = part + out_low
                if (b + s) * BLOCK >= HALF + nodes:
                    part = part + out_high
                parts.append(part)
            top = functools.reduce(jnp.maximum, parts)
            top = jnp.max(top, -1, keepdims=True)
            weight = jnp.concatenate([jnp.exp(part - top).astype(bf16) for part in parts], 1)
            mixed = dot(weight, jnp.concatenate([values[window, cols], ones], 1))
            mixed = mixed[:, :LANES] / mixed[:, LANES:]
            attended[rows, cols] = jnp.where(first_head, mixed[:BLOCK], mixed[BLOCK:]).astype(bf16)


def mine_kernel(
    edge, before, feats, after, gain, gathered_weights, scale,
    attended, normed,
    weights, query, keys, values, sems,
):
    copies = weight_copies(gathered_weights, weights, sems)
    for copy in copies:
        copy.start()
    normalise(before, feats, after, gain, normed)
    for copy in copies:
        copy.wait()
    base = edge[2] * (scale.shape[1] // 2)
    attend_pairs(edge, normed, weights, scale, base, query, keys, values, attended)


def other_kernel(
    edge, normed, gathered_weights, scale,
    attended,
    weights, query, keys, values, sems,
):
    copies = weight_copies(gathered_weights, weights, sems)
    for copy in copies:
        copy.start()
    for copy in copies:
        copy.wait()
    base = (1 - edge[2]) * (scale.shape[1] // 2)
    attend_pairs(edge, normed, weights, scale, base, query, keys, values, attended)


def hidden_kernel(
    edge, feats, attended_mine, attended_other, gathered_mine, gathered_other, w_dec,
    hidden_out, fields_out,
    out_mine, out_other, sems_mine, sems_other,
):
    nodes, width = feats.shape
    mine = width // 2
    copies = weight_copies(gathered_mine, out_mine, sems_mine)
    copies += weight_copies(gathered_other, out_other, sems_other)
    for copy in copies:
        copy.start()
    here = pl.ds(pl.multiple_of(edge[2] * mine, mine), mine)
    there = pl.ds(pl.multiple_of((1 - edge[2]) * mine, mine), mine)
    for copy in copies:
        copy.wait()
    for half, cols in ((out_mine, here), (out_other, there)):
        flat = half.reshape(width, mine)
        for r in range(nodes // 256):
            rows = pl.ds(r * 256, 256)
            projected = dot(attended_mine[rows, :], flat[here, :]) + dot(attended_other[rows, :], flat[there, :])
            hidden_out[rows, cols] = (feats[rows, cols].astype(f32) + projected).astype(bf16)
    fields_out[...] = dot_t(w_dec[...], hidden_out[...]).astype(bf16)


def score_kernel(
    own, same_core, other_core, hidden, targets, cell_node, cell_area,
    score_out, grad_out,
):
    members = 2 * same_core.shape[0]
    nodes = own.shape[1]
    variables, cells = targets.shape
    mine = own[...].astype(f32)
    spread = jnp.zeros_like(mine) - SMOOTH_SQ**0.5
    slope = jnp.zeros_like(mine)
    for ref in (same_core, other_core):
        for j in range(members // 2):
            delta = mine - ref[j].astype(f32)
            square = delta * delta + SMOOTH_SQ
            inverse = lax.rsqrt(square)
            spread = spread + square * inverse
            slope = slope + delta * inverse
    kappa = ALPHA / (2.0 * members * (members - 1)) + (1.0 - ALPHA) / (2.0 * members * members)
    index = lax.broadcasted_iota(jnp.int32, (nodes, cells), 0)
    one_hot = (index == cell_node[...]).astype(bf16)
    high, low = halves(spread)
    fields = dot(own[...], one_hot)
    spread = dot(high, one_hot) + dot(low, one_hot)
    error = fields - targets[...].astype(f32)
    square = error * error + SMOOTH_SQ
    inverse = lax.rsqrt(square)
    score_out[...] = square * inverse * (1.0 / members) - kappa * spread
    area = cell_area[...]
    high, low = halves(area * (error * inverse) * (1.0 / members))
    area_high, area_low = halves(jnp.broadcast_to(area, (8, cells)))
    node_grad = dot_t(high, one_hot) + dot_t(low, one_hot)
    node_area = dot_t(area_high, one_hot) + dot_t(area_low, one_hot)
    node_grad = node_grad - (2.0 * kappa) * slope * node_area[:1]
    grad = dot(node_grad.astype(bf16), hidden[...])
    tiles = grad.shape[1] // LANES
    each = grad_out.shape[1] // 16
    grad = jnp.concatenate([grad, jnp.zeros((128 - variables, grad.shape[1]), f32)], 0).astype(bf16)
    for r in range(128 // 16):
        for c in range(tiles):
            tile = r * tiles + c
            grad_out[tile // each, pl.ds(tile % each * 16, 16), :] = grad[
                r * 16 : r * 16 + 16, c * LANES : (c + 1) * LANES
            ]


def shifted(value, axis, steps):
    count = lax.axis_size(axis)
    return lax.ppermute(value, axis, [(i, (i + steps) % count) for i in range(count)])


def gathered(x, axis):
    count = lax.axis_size(axis)
    return lax.all_to_all(jnp.broadcast_to(x[None], (count,) + x.shape), axis, 0, 0)


def total(pieces):
    piece = jnp.sum(lax.all_to_all(pieces, PLANE, 0, 0).astype(f32), 0)
    piece = jnp.sum(gathered(piece.astype(bf16), LINE).astype(f32), 0)
    return gathered(piece.astype(bf16), PLANE).astype(f32)


def body(
    node_feats, norm_gain, w_query, w_key, w_value, w_out, head_scale, w_dec, targets, cell_node, cell_area
):
    feats = node_feats[0]
    nodes, width = feats.shape
    ext = nodes + 2 * HALF
    shards = lax.axis_size(GRID)
    core = lax.axis_index("core")
    variables = w_dec.shape[0]
    up = [(i, i + 1) for i in range(shards - 1)]
    before = lax.ppermute(feats[nodes - HALF :], GRID, up)
    after = lax.ppermute(feats[:HALF], GRID, [(j, i) for i, j in up])

    mine = width // 2
    rows = w_query.shape[0]
    parts = [
        lax.dynamic_slice_in_dim(w, core * mine, mine, 1) for w in (w_query, w_key, w_value, w_out)
    ]
    by_pair = jnp.stack([w.reshape(rows, mine // LANES, LANES) for w in parts[:3]], 2)
    shard = jnp.concatenate([by_pair.reshape(rows, 3 * mine), parts[3]], 1)
    lane = gathered(shard, "z_lo")
    grouped = lambda w: w.reshape((lax.axis_size("y"), lax.axis_size("x")) + w.shape[1:])
    heads_mine = gathered(lane[..., : 3 * mine], ("y", "x"))
    heads_mine, before, after, lane_out = lax.optimization_barrier(
        (heads_mine, before, after, lane[..., 3 * mine :])
    )
    heads_mine = grouped(heads_mine)
    out_mine = grouped(gathered(lane_out, ("y", "x")))
    heads_other = shifted(heads_mine, "core", 1)

    scale = jnp.repeat(head_scale, width // head_scale.shape[0])[None]
    edge = jnp.stack([lax.axis_index(GRID), jnp.int32(shards), core]).astype(jnp.int32)
    smem = pl.BlockSpec(memory_space=pltpu.SMEM)
    vmem = pl.BlockSpec(memory_space=pltpu.VMEM)
    anywhere = pl.BlockSpec(memory_space=pl.ANY)
    params = pltpu.CompilerParams(vmem_limit_bytes=28 * MIB)
    groups = shards // lax.axis_size("x")
    weights = lambda n: pltpu.VMEM((groups, shards // groups, rows, n), bf16)
    sems = pltpu.SemaphoreType.DMA((groups,))
    heads = [pltpu.VMEM((n, mine), bf16) for n in (nodes, ext, ext)]
    cost = pl.CostEstimate(flops=4_000_000_000, bytes_accessed=8_000_000, transcendentals=0)
    half = jax.ShapeDtypeStruct((nodes, mine), bf16)
    attended_mine, normed = pl.pallas_call(
        mine_kernel,
        out_shape=(half, jax.ShapeDtypeStruct((ext, width), bf16)),
        in_specs=[smem] + [vmem] * 4 + [anywhere, vmem],
        out_specs=(vmem, vmem),
        scratch_shapes=[weights(3 * mine), *heads, sems],
        compiler_params=params,
        cost_estimate=cost,
        name="heads_mine",
    )(edge, before, feats, after, norm_gain[None], heads_mine, scale)
    attended_other = pl.pallas_call(
        other_kernel,
        out_shape=half,
        in_specs=[smem, vmem, anywhere, vmem],
        out_specs=vmem,
        scratch_shapes=[weights(3 * mine), *heads, sems],
        compiler_params=params,
        cost_estimate=cost,
        name="heads_other",
    )(edge, normed, heads_other, scale)
    out_mine, attended_mine = lax.optimization_barrier((out_mine, attended_mine))
    out_other = shifted(out_mine, "core", 1)
    hidden, fields = pl.pallas_call(
        hidden_kernel,
        out_shape=(
            jax.ShapeDtypeStruct((nodes, width), bf16),
            jax.ShapeDtypeStruct((variables, nodes), bf16),
        ),
        in_specs=[smem, vmem, vmem, vmem, anywhere, anywhere, vmem],
        out_specs=(vmem, vmem),
        scratch_shapes=[weights(mine), weights(mine), sems, sems],
        compiler_params=params,
        name="hidden",
    )(edge, feats, attended_mine, attended_other, out_mine, out_other, w_dec)

    same_core = gathered(fields, "z_hi")
    other_core = shifted(same_core, "core", 1)
    pieces = lax.axis_size(PLANE)
    score, grad = pl.pallas_call(
        score_kernel,
        out_shape=(
            jax.ShapeDtypeStruct(targets.shape, f32),
            jax.ShapeDtypeStruct((pieces, width // pieces, LANES), bf16),
        ),
        in_specs=[vmem] * 7,
        out_specs=(vmem, vmem),
        compiler_params=params,
        name="score",
    )(fields, same_core, other_core, hidden, targets, cell_node[None], cell_area[None])
    grad = total(grad).reshape(8, width // LANES, 16, LANES).transpose(0, 2, 1, 3)
    return score[None], grad.reshape(128, width)[:variables]


def solution(mesh):
    fine = Mesh(mesh.devices.reshape(4, 2, 4, 4, 4), MEMBER + GRID)
    in_specs = (
        P(MEMBER, GRID, None),
        P(),
        P(GRID, None),
        P(GRID, None),
        P(GRID, None),
        P(GRID, None),
        P(),
        P(),
        P(None, GRID),
        P(GRID),
        P(GRID),
    )
    out_specs = (P(MEMBER, None, GRID), P())
    return jax.shard_map(body, mesh=fine, in_specs=in_specs, out_specs=out_specs, check_vma=False)
```

```python
import functools

import jax
import jax.numpy as jnp
from jax import lax
from jax.experimental import pallas as pl
from jax.experimental.pallas import tpu as pltpu
from jax.sharding import Mesh, PartitionSpec as P

HALF = 256
EPS = 1e-06
SMOOTH_SQ = 0.0625
ALPHA = 0.95
LANES = 128
BLOCK = 128
LOW = -1e30
MIB = 1024 * 1024
EARLY = 3

GRID = ("y", "z_lo", "x")
MEMBER = ("z_hi", "core")
PLANE = ("core", "y", "x")
LINE = ("z_hi", "z_lo")

f32 = jnp.float32
bf16 = jnp.bfloat16


def dot(a, b):
    return jnp.dot(a, b, preferred_element_type=f32)


def dot_t(a, b):
    return lax.dot_general(a, b, (((1,), (1,)), ((), ())), preferred_element_type=f32)


def halves(x):
    high = x.astype(bf16)
    return high, (x - high.astype(f32)).astype(bf16)


def loop(count, fn):
    def step(i, _):
        fn(i)
        return 0

    lax.fori_loop(0, count, step, 0)


def normalise(before, feats, after, gain, normed):
    gain_row = gain[...].astype(f32)
    start = 0
    for ref in (before, feats, after):

        def norm(i, ref=ref, start=start):
            x = ref[pl.ds(pl.multiple_of(i * 64, 64), 64), :].astype(f32)
            mean = jnp.mean(x * x, -1, keepdims=True)
            y = x * lax.rsqrt(mean + EPS) * gain_row
            normed[pl.ds(pl.multiple_of(start + i * 64, 64), 64), :] = y.astype(bf16)

        loop(ref.shape[0] // 64, norm)
        start += ref.shape[0]


def lane_tiles(x):
    whole = x.shape[0] // 16 * 16
    tiles = [x[:, t * LANES : (t + 1) * LANES] for t in range(x.shape[1] // LANES)]
    return [tile[:whole] for tile in tiles], jnp.concatenate([tile[whole:] for tile in tiles], 0)


def from_lane_tiles(tiles, rest):
    each = rest.shape[0] // len(tiles)
    whole = [
        jnp.concatenate([tile, rest[t * each : (t + 1) * each]], 0) for t, tile in enumerate(tiles)
    ]
    return jnp.concatenate(whole, 1)


def weight_copies(gathered_weights, weights, sems):
    ys, xs, zs, rows, _ = gathered_weights.shape
    copies = []
    for y in range(ys):
        for z in range(zs):
            copies.append(
                pltpu.make_async_copy(
                    gathered_weights.at[y, :, z], weights.at[y * zs + z], sems.at[y * zs + z]
                )
            )
    return copies


def attend_pairs(edge, normed, weights, scale, half, first, query, keys, values, attended):
    base = half * (scale.shape[1] // 2) + first * LANES
    ext, width = normed.shape
    nodes = ext - 2 * HALF
    pairs = weights.shape[-1] // (3 * LANES)
    flat = weights.reshape(width, weights.shape[-1])

    def unit(y):
        first_head = lax.broadcasted_iota(jnp.int32, y.shape, 1) < 64
        square = y * y
        first = jnp.sum(jnp.where(first_head, square, 0.0), -1, keepdims=True)
        second = jnp.sum(jnp.where(first_head, 0.0, square), -1, keepdims=True)
        return y * lax.rsqrt(jnp.where(first_head, first, second) + EPS)

    for p in range(pairs):
        cols = pl.ds(p * LANES, LANES)
        query_cols = pl.ds(p * 3 * LANES, LANES)
        keyval_cols = pl.ds(p * 3 * LANES + LANES, 2 * LANES)
        factor = scale[:, pl.ds(pl.multiple_of(base + p * LANES, LANES), LANES)]
        for r in range(nodes // 256):
            rows = pl.ds(r * 256, 256)
            y = dot(normed[pl.ds(HALF + r * 256, 256), :], flat[:, query_cols])
            query[rows, cols] = (unit(y) * factor).astype(bf16)
        for r in range(ext // 256):
            rows = pl.ds(r * 256, 256)
            y = dot(normed[rows, :], flat[:, keyval_cols])
            keys[rows, cols] = unit(y[:, :LANES]).astype(bf16)
            values[rows, cols] = y[:, LANES:].astype(bf16)

    row = lax.broadcasted_iota(jnp.int32, (2 * BLOCK, BLOCK), 0) % BLOCK
    col = lax.broadcasted_iota(jnp.int32, (2 * BLOCK, BLOCK), 1)
    lead = jnp.where(col >= row, 0.0, LOW).astype(f32)
    tail = jnp.where(col < row, 0.0, LOW).astype(f32)
    first_head = lax.broadcasted_iota(jnp.int32, (BLOCK, LANES), 1) < 64
    ones = jnp.ones((2 * HALF + BLOCK, LANES), bf16)
    segments = 2 * HALF // BLOCK + 1
    out_low = jnp.where(edge[0] == 0, LOW, 0.0).astype(f32)
    out_high = jnp.where(edge[0] == edge[1] - 1, LOW, 0.0).astype(f32)
    for p in range(pairs):
        cols = pl.ds(p * LANES, LANES)
        for b in range(nodes // BLOCK):
            rows = pl.ds(b * BLOCK, BLOCK)
            window = pl.ds(b * BLOCK, 2 * HALF + BLOCK)
            q = query[rows, cols]
            zero = jnp.zeros_like(q)
            pair = jnp.concatenate([jnp.where(first_head, q, zero), jnp.where(first_head, zero, q)], 0)
            score = dot_t(pair, keys[window, cols])
            parts = []
            for s in range(segments):
                part = score[:, s * BLOCK : (s + 1) * BLOCK]
                if s == 0:
                    part = part + lead
                if s == segments - 1:
                    part = part + tail
                if (b + s + 1) * BLOCK <= HALF:
                    part = part + out_low
                if (b + s) * BLOCK >= HALF + nodes:
                    part = part + out_high
                parts.append(part)
            top = functools.reduce(jnp.maximum, parts)
            top = jnp.max(top, -1, keepdims=True)
            weight = jnp.concatenate([jnp.exp(part - top).astype(bf16) for part in parts], 1)
            mixed = dot(weight, jnp.concatenate([values[window, cols], ones], 1))
            mixed = mixed[:, :LANES] / mixed[:, LANES:]
            out_cols = pl.ds(pl.multiple_of(base + p * LANES, LANES), LANES)
            attended[rows, out_cols] = jnp.where(first_head, mixed[:BLOCK], mixed[BLOCK:]).astype(bf16)


def early_kernel(
    edge, before, feats, after, gain, gathered_mine, gathered_other, scale,
    attended, normed_out,
    normed, weights_mine, weights_other, query, keys, values, sems_mine, sems_other, out_sem,
):
    copies_mine = weight_copies(gathered_mine, weights_mine, sems_mine)
    copies_other = weight_copies(gathered_other, weights_other, sems_other)
    for copy in copies_mine + copies_other:
        copy.start()
    normalise(before, feats, after, gain, normed)
    leave = pltpu.make_async_copy(normed, normed_out, out_sem)
    leave.start()
    for i, (half, weights, copies) in enumerate(
        ((edge[2], weights_mine, copies_mine), (1 - edge[2], weights_other, copies_other))
    ):
        for copy in copies:
            copy.wait()
        attend_pairs(edge, normed, weights, scale, half, 0, query.at[i], keys.at[i], values.at[i], attended)
    leave.wait()


def late_kernel(
    edge, feats, normed_in, attended_early, gathered_mine, gathered_other, scale, w_dec,
    hidden_out, fields_out, packed_out,
    normed, attended, weights_mine, weights_other, out_mine, out_other, query, keys, values,
    in_sem, sems_mine, sems_other, sems_out_mine, sems_out_other,
):
    nodes, width = feats.shape
    mine = width // 2
    columns = weights_mine.shape[-1]
    heads, out = pl.ds(0, columns), pl.ds(columns, mine)
    enter = pltpu.make_async_copy(normed_in, normed, in_sem)
    copies_mine = weight_copies(gathered_mine.at[..., heads], weights_mine, sems_mine)
    copies_other = weight_copies(gathered_other.at[..., heads], weights_other, sems_other)
    copies_out = weight_copies(gathered_mine.at[..., out], out_mine, sems_out_mine)
    copies_out += weight_copies(gathered_other.at[..., out], out_other, sems_out_other)
    for copy in [enter] + copies_mine + copies_other + copies_out:
        copy.start()
    attended[...] = attended_early[...]
    enter.wait()
    for i, (half, weights, copies) in enumerate(
        ((edge[2], weights_mine, copies_mine), (1 - edge[2], weights_other, copies_other))
    ):
        for copy in copies:
            copy.wait()
        attend_pairs(edge, normed, weights, scale, half, EARLY, query.at[i], keys.at[i], values.at[i], attended)
    here = pl.ds(pl.multiple_of(edge[2] * mine, mine), mine)
    there = pl.ds(pl.multiple_of((1 - edge[2]) * mine, mine), mine)
    for copy in copies_out:
        copy.wait()
    for half, cols in ((out_mine, here), (out_other, there)):
        flat = half.reshape(width, mine)
        for r in range(nodes // 256):
            rows = pl.ds(r * 256, 256)
            hidden = feats[rows, cols].astype(f32) + dot(attended[rows, :], flat[...])
            hidden_out[rows, cols] = hidden.astype(bf16)
    fields = dot_t(w_dec[...], hidden_out[...])
    fields_out[...] = fields.astype(bf16)
    tiles, rest = lane_tiles(fields)
    blocks = tiles[0].shape[0] // 16
    for t, tile in enumerate(tiles):
        for i in range(blocks):
            packed_out[t * blocks + i] = tile[i * 16 : i * 16 + 16].astype(bf16)
    packed_out[len(tiles) * blocks] = rest.astype(bf16)


def score_kernel(
    own, same_core, other_core, hidden, targets, cell_node, cell_area,
    score_out, grad_out,
):
    members = 2 * same_core.shape[0]
    nodes = own.shape[1]
    variables, cells = targets.shape
    tiles, rest = lane_tiles(own[...].astype(f32))
    blocks = tiles[0].shape[0] // 16
    spreads, slopes = [], []
    for t, mine in enumerate(tiles + [rest]):
        spread = jnp.zeros_like(mine) - SMOOTH_SQ**0.5
        slope = jnp.zeros_like(mine)
        for ref in (same_core, other_core):
            for j in range(members // 2):
                if t < len(tiles):
                    other = ref[j, t * blocks : (t + 1) * blocks].reshape(mine.shape)
                else:
                    other = ref[j, t * blocks]
                delta = mine - other.astype(f32)
                square = delta * delta + SMOOTH_SQ
                inverse = lax.rsqrt(square)
                spread = spread + square * inverse
                slope = slope + delta * inverse
        spreads.append(spread)
        slopes.append(slope)
    spread = from_lane_tiles(spreads[:-1], spreads[-1])
    slope = from_lane_tiles(slopes[:-1], slopes[-1])
    kappa = ALPHA / (2.0 * members * (members - 1)) + (1.0 - ALPHA) / (2.0 * members * members)
    index = lax.broadcasted_iota(jnp.int32, (nodes, cells), 0)
    one_hot = (index == cell_node[...]).astype(bf16)
    high, low = halves(spread)
    fields = dot(own[...], one_hot)
    spread = dot(high, one_hot) + dot(low, one_hot)
    error = fields - targets[...].astype(f32)
    square = error * error + SMOOTH_SQ
    inverse = lax.rsqrt(square)
    score_out[...] = square * inverse * (1.0 / members) - kappa * spread
    area = cell_area[...]
    high, low = halves(area * (error * inverse) * (1.0 / members))
    area_high, area_low = halves(jnp.broadcast_to(area, (8, cells)))
    node_grad = dot_t(high, one_hot) + dot_t(low, one_hot)
    node_area = dot_t(area_high, one_hot) + dot_t(area_low, one_hot)
    node_grad = node_grad - (2.0 * kappa) * slope * node_area[:1]
    grad = dot(node_grad.astype(bf16), hidden[...])
    tiles = grad.shape[1] // LANES
    each = grad_out.shape[1] // 16
    grad = jnp.concatenate([grad, jnp.zeros((128 - variables, grad.shape[1]), f32)], 0).astype(bf16)
    for r in range(128 // 16):
        for c in range(tiles):
            tile = r * tiles + c
            grad_out[tile // each, pl.ds(tile % each * 16, 16), :] = grad[
                r * 16 : r * 16 + 16, c * LANES : (c + 1) * LANES
            ]


def shifted(value, axis, steps):
    count = lax.axis_size(axis)
    return lax.ppermute(value, axis, [(i, (i + steps) % count) for i in range(count)])


def copies_for(x, axis):
    return jnp.broadcast_to(x[None], (lax.axis_size(axis),) + x.shape)


def gathered(x, axis):
    return lax.all_to_all(copies_for(x, axis), axis, 0, 0)


def total(pieces):
    piece = jnp.sum(lax.all_to_all(pieces, PLANE, 0, 0).astype(f32), 0)
    piece = jnp.sum(gathered(piece.astype(bf16), LINE).astype(f32), 0)
    return gathered(piece.astype(bf16), PLANE).astype(f32)


def body(
    node_feats, norm_gain, w_query, w_key, w_value, w_out, head_scale, w_dec, targets, cell_node, cell_area
):
    feats = node_feats[0]
    nodes, width = feats.shape
    ext = nodes + 2 * HALF
    shards = lax.axis_size(GRID)
    core = lax.axis_index("core")
    variables = w_dec.shape[0]
    up = [(i, i + 1) for i in range(shards - 1)]
    before = lax.ppermute(feats[nodes - HALF :], GRID, up)
    after = lax.ppermute(feats[:HALF], GRID, [(j, i) for i, j in up])

    mine = width // 2
    rows = w_query.shape[0]
    parts = [
        lax.dynamic_slice_in_dim(w, core * mine, mine, 1) for w in (w_query, w_key, w_value, w_out)
    ]
    by_pair = jnp.stack([w.reshape(rows, mine // LANES, LANES) for w in parts[:3]], 2)
    shard = jnp.concatenate([by_pair.reshape(rows, 3 * mine), parts[3]], 1)
    lane = gathered(shard, "z_lo")
    plane = gathered(lane, "x")
    late = mine // LANES - EARLY
    cut = EARLY * 3 * LANES
    early_mine = gathered(plane[..., :cut], "y")
    early_mine, before, after, plane_late = lax.optimization_barrier(
        (early_mine, before, after, copies_for(plane[..., cut:], "y"))
    )
    late_mine = lax.all_to_all(plane_late, "y", 0, 0)
    early_other = shifted(early_mine, "core", 1)

    scale = jnp.repeat(head_scale, width // head_scale.shape[0])[None]
    edge = jnp.stack([lax.axis_index(GRID), jnp.int32(shards), core]).astype(jnp.int32)
    smem = pl.BlockSpec(memory_space=pltpu.SMEM)
    vmem = pl.BlockSpec(memory_space=pltpu.VMEM)
    anywhere = pl.BlockSpec(memory_space=pl.ANY)
    params = pltpu.CompilerParams(vmem_limit_bytes=28 * MIB)
    groups = shards // lax.axis_size("x")
    weights = lambda n: pltpu.VMEM((groups, shards // groups, rows, n), bf16)
    sem, sems = pltpu.SemaphoreType.DMA, pltpu.SemaphoreType.DMA((groups,))
    extended = pltpu.VMEM((ext, width), bf16)
    heads = lambda n: [pltpu.VMEM((2, k, n * LANES), bf16) for k in (nodes, ext, ext)]
    whole = jax.ShapeDtypeStruct((nodes, width), bf16)
    attended, normed = pl.pallas_call(
        early_kernel,
        out_shape=(whole, jax.ShapeDtypeStruct((ext, width), bf16)),
        in_specs=[smem] + [vmem] * 4 + [anywhere, anywhere, vmem],
        out_specs=(vmem, anywhere),
        scratch_shapes=[extended, weights(cut), weights(cut), *heads(EARLY), sems, sems, sem],
        compiler_params=params,
        cost_estimate=pl.CostEstimate(flops=8_000_000_000, bytes_accessed=16_000_000, transcendentals=0),
        name="early_heads",
    )(edge, before, feats, after, norm_gain[None], early_mine, early_other, scale)
    late_mine, attended = lax.optimization_barrier((late_mine, attended))
    late_other = shifted(late_mine, "core", 1)
    hidden, fields, packed = pl.pallas_call(
        late_kernel,
        out_shape=(
            whole,
            jax.ShapeDtypeStruct((variables, nodes), bf16),
            jax.ShapeDtypeStruct((variables * nodes // (16 * LANES), 16, LANES), bf16),
        ),
        in_specs=[smem, vmem, anywhere, vmem, anywhere, anywhere, vmem, vmem],
        out_specs=(vmem, vmem, vmem),
        scratch_shapes=[
            extended,
            pltpu.VMEM((nodes, width), bf16),
            weights(late * 3 * LANES),
            weights(late * 3 * LANES),
            weights(mine),
            weights(mine),
            *heads(late),
            sem,
            sems,
            sems,
            sems,
            sems,
        ],
        compiler_params=params,
        name="late_heads",
    )(edge, feats, normed, attended, late_mine, late_other, scale, w_dec)

    same_core = gathered(packed, "z_hi")
    other_core = shifted(same_core, "core", 1)
    pieces = lax.axis_size(PLANE)
    score, grad = pl.pallas_call(
        score_kernel,
        out_shape=(
            jax.ShapeDtypeStruct(targets.shape, f32),
            jax.ShapeDtypeStruct((pieces, width // pieces, LANES), bf16),
        ),
        in_specs=[vmem] * 7,
        out_specs=(vmem, vmem),
        compiler_params=params,
        name="score",
    )(fields, same_core, other_core, hidden, targets, cell_node[None], cell_area[None])
    grad = total(grad).reshape(8, width // LANES, 16, LANES).transpose(0, 2, 1, 3)
    return score[None], grad.reshape(128, width)[:variables]


def solution(mesh):
    fine = Mesh(mesh.devices.reshape(4, 2, 4, 4, 4), MEMBER + GRID)
    in_specs = (
        P(MEMBER, GRID, None),
        P(),
        P(GRID, None),
        P(GRID, None),
        P(GRID, None),
        P(GRID, None),
        P(),
        P(),
        P(None, GRID),
        P(GRID),
        P(GRID),
    )
    out_specs = (P(MEMBER, None, GRID), P())
    return jax.shard_map(body, mesh=fine, in_specs=in_specs, out_specs=out_specs, check_vma=False)
```

```python
import functools

import jax
import jax.numpy as jnp
from jax import lax
from jax.experimental import pallas as pl
from jax.experimental.pallas import tpu as pltpu
from jax.sharding import Mesh, PartitionSpec as P

HALF = 256
EPS = 1e-06
SMOOTH_SQ = 0.0625
ALPHA = 0.95
LANES = 128
BLOCK = 128
LOW = -1e30
MIB = 1024 * 1024
EARLY = 3
SKEW = 2

GRID = ("y", "z_lo", "x")
MEMBER = ("z_hi", "core")
PLANE = ("core", "y", "x")
LINE = ("z_hi", "z_lo")

f32 = jnp.float32
bf16 = jnp.bfloat16


def dot(a, b):
    return jnp.dot(a, b, preferred_element_type=f32)


def dot_t(a, b):
    return lax.dot_general(a, b, (((1,), (1,)), ((), ())), preferred_element_type=f32)


def halves(x):
    high = x.astype(bf16)
    return high, (x - high.astype(f32)).astype(bf16)


def loop(count, fn):
    def step(i, _):
        fn(i)
        return 0

    lax.fori_loop(0, count, step, 0)


def normalise(before, feats, after, gain, normed):
    gain_row = gain[...].astype(f32)
    start = 0
    for ref in (before, feats, after):

        def norm(i, ref=ref, start=start):
            x = ref[pl.ds(pl.multiple_of(i * 64, 64), 64), :].astype(f32)
            mean = jnp.mean(x * x, -1, keepdims=True)
            y = x * lax.rsqrt(mean + EPS) * gain_row
            normed[pl.ds(pl.multiple_of(start + i * 64, 64), 64), :] = y.astype(bf16)

        loop(ref.shape[0] // 64, norm)
        start += ref.shape[0]


def lane_tiles(x):
    whole = x.shape[0] // 16 * 16
    tiles = [x[:, t * LANES : (t + 1) * LANES] for t in range(x.shape[1] // LANES)]
    return [tile[:whole] for tile in tiles], jnp.concatenate([tile[whole:] for tile in tiles], 0)


def from_lane_tiles(tiles, rest):
    each = rest.shape[0] // len(tiles)
    whole = [
        jnp.concatenate([tile, rest[t * each : (t + 1) * each]], 0) for t, tile in enumerate(tiles)
    ]
    return jnp.concatenate(whole, 1)


def weight_copies(gathered_weights, weights, sems):
    ys, xs, zs, rows, _ = gathered_weights.shape
    copies = []
    for y in range(ys):
        for z in range(zs):
            copies.append(
                pltpu.make_async_copy(
                    gathered_weights.at[y, :, z], weights.at[y * zs + z], sems.at[y * zs + z]
                )
            )
    return copies


def attend_pairs(edge, normed, weights, scale, half, first, query, keys, values, attended):
    base = half * (scale.shape[1] // 2) + first * LANES
    ext, width = normed.shape
    nodes = ext - 2 * HALF
    pairs = weights.shape[-1] // (3 * LANES)
    flat = weights.reshape(width, weights.shape[-1])

    def unit(y):
        first_head = lax.broadcasted_iota(jnp.int32, y.shape, 1) < 64
        square = y * y
        first = jnp.sum(jnp.where(first_head, square, 0.0), -1, keepdims=True)
        second = jnp.sum(jnp.where(first_head, 0.0, square), -1, keepdims=True)
        return y * lax.rsqrt(jnp.where(first_head, first, second) + EPS)

    def project(p):
        cols = pl.ds(p * LANES, LANES)
        query_cols = pl.ds(p * 3 * LANES, LANES)
        keyval_cols = pl.ds(p * 3 * LANES + LANES, 2 * LANES)
        factor = scale[:, pl.ds(pl.multiple_of(base + p * LANES, LANES), LANES)]
        for r in range(nodes // 256):
            rows = pl.ds(r * 256, 256)
            y = dot(normed[pl.ds(HALF + r * 256, 256), :], flat[:, query_cols])
            query[rows, cols] = (unit(y) * factor).astype(bf16)
        for r in range(ext // 256):
            rows = pl.ds(r * 256, 256)
            y = dot(normed[rows, :], flat[:, keyval_cols])
            keys[rows, cols] = unit(y[:, :LANES]).astype(bf16)
            values[rows, cols] = y[:, LANES:].astype(bf16)

    row = lax.broadcasted_iota(jnp.int32, (2 * BLOCK, BLOCK), 0) % BLOCK
    col = lax.broadcasted_iota(jnp.int32, (2 * BLOCK, BLOCK), 1)
    lead = jnp.where(col >= row, 0.0, LOW).astype(f32)
    tail = jnp.where(col < row, 0.0, LOW).astype(f32)
    first_head = lax.broadcasted_iota(jnp.int32, (BLOCK, LANES), 1) < 64
    ones = jnp.ones((2 * HALF + BLOCK, LANES), bf16)
    segments = 2 * HALF // BLOCK + 1
    blocks = nodes // BLOCK
    out_low = jnp.where(edge[0] == 0, LOW, 0.0).astype(f32)
    out_high = jnp.where(edge[0] == edge[1] - 1, LOW, 0.0).astype(f32)

    def scores(p, b):
        cols = pl.ds(p * LANES, LANES)
        q = query[pl.ds(b * BLOCK, BLOCK), cols]
        zero = jnp.zeros_like(q)
        pair = jnp.concatenate([jnp.where(first_head, q, zero), jnp.where(first_head, zero, q)], 0)
        score = dot_t(pair, keys[pl.ds(b * BLOCK, 2 * HALF + BLOCK), cols])
        parts = []
        for s in range(segments):
            part = score[:, s * BLOCK : (s + 1) * BLOCK]
            if s == 0:
                part = part + lead
            if s == segments - 1:
                part = part + tail
            if (b + s + 1) * BLOCK <= HALF:
                part = part + out_low
            if (b + s) * BLOCK >= HALF + nodes:
                part = part + out_high
            parts.append(part)
        return parts

    def softened(parts):
        top = functools.reduce(jnp.maximum, parts)
        top = jnp.max(top, -1, keepdims=True)
        return jnp.concatenate([jnp.exp(part - top).astype(bf16) for part in parts], 1)

    def mix(p, b, weight):
        window = pl.ds(b * BLOCK, 2 * HALF + BLOCK)
        value = values[window, pl.ds(p * LANES, LANES)]
        mixed = dot(weight, jnp.concatenate([value, ones], 1))
        mixed = mixed[:, :LANES] / mixed[:, LANES:]
        out_cols = pl.ds(pl.multiple_of(base + p * LANES, LANES), LANES)
        attended[pl.ds(b * BLOCK, BLOCK), out_cols] = jnp.where(
            first_head, mixed[:BLOCK], mixed[BLOCK:]
        ).astype(bf16)

    items = [(p, b) for p in range(pairs) for b in range(blocks)]
    score, weight = {}, {}
    project(0)
    for i in range(len(items) + 2 * SKEW):
        if i < len(items):
            if i % blocks == 0 and i // blocks + 1 < pairs:
                project(i // blocks + 1)
            score[i] = scores(*items[i])
        j = i - SKEW
        if 0 <= j < len(items):
            weight[j] = softened(score.pop(j))
        k = j - SKEW
        if 0 <= k < len(items):
            mix(*items[k], weight.pop(k))


def early_kernel(
    edge, before, feats, after, gain, gathered_mine, gathered_other, scale,
    attended, normed_out,
    normed, weights_mine, weights_other, query, keys, values, sems_mine, sems_other, out_sem,
):
    copies_mine = weight_copies(gathered_mine, weights_mine, sems_mine)
    copies_other = weight_copies(gathered_other, weights_other, sems_other)
    for copy in copies_mine + copies_other:
        copy.start()
    normalise(before, feats, after, gain, normed)
    leave = pltpu.make_async_copy(normed, normed_out, out_sem)
    leave.start()
    for i, (half, weights, copies) in enumerate(
        ((edge[2], weights_mine, copies_mine), (1 - edge[2], weights_other, copies_other))
    ):
        for copy in copies:
            copy.wait()
        attend_pairs(edge, normed, weights, scale, half, 0, query.at[i], keys.at[i], values.at[i], attended)
    leave.wait()


def late_kernel(
    edge, feats, normed_in, attended_early, gathered_mine, gathered_other, scale, w_dec,
    hidden_out, fields_out, packed_out,
    normed, attended, weights_mine, weights_other, out_mine, out_other, query, keys, values,
    in_sem, sems_mine, sems_other, sems_out_mine, sems_out_other,
):
    nodes, width = feats.shape
    mine = width // 2
    columns = weights_mine.shape[-1]
    heads, out = pl.ds(0, columns), pl.ds(columns, mine)
    enter = pltpu.make_async_copy(normed_in, normed, in_sem)
    copies_mine = weight_copies(gathered_mine.at[..., heads], weights_mine, sems_mine)
    copies_other = weight_copies(gathered_other.at[..., heads], weights_other, sems_other)
    copies_out = weight_copies(gathered_mine.at[..., out], out_mine, sems_out_mine)
    copies_out += weight_copies(gathered_other.at[..., out], out_other, sems_out_other)
    for copy in [enter] + copies_mine + copies_other + copies_out:
        copy.start()
    attended[...] = attended_early[...]
    enter.wait()
    for i, (half, weights, copies) in enumerate(
        ((edge[2], weights_mine, copies_mine), (1 - edge[2], weights_other, copies_other))
    ):
        for copy in copies:
            copy.wait()
        attend_pairs(edge, normed, weights, scale, half, EARLY, query.at[i], keys.at[i], values.at[i], attended)
    here = pl.ds(pl.multiple_of(edge[2] * mine, mine), mine)
    there = pl.ds(pl.multiple_of((1 - edge[2]) * mine, mine), mine)
    for copy in copies_out:
        copy.wait()
    for half, cols in ((out_mine, here), (out_other, there)):
        flat = half.reshape(width, mine)
        for r in range(nodes // 256):
            rows = pl.ds(r * 256, 256)
            hidden = feats[rows, cols].astype(f32) + dot(attended[rows, :], flat[...])
            hidden_out[rows, cols] = hidden.astype(bf16)
    fields = dot_t(w_dec[...], hidden_out[...])
    fields_out[...] = fields.astype(bf16)
    tiles, rest = lane_tiles(fields)
    blocks = tiles[0].shape[0] // 16
    for t, tile in enumerate(tiles):
        for i in range(blocks):
            packed_out[t * blocks + i] = tile[i * 16 : i * 16 + 16].astype(bf16)
    packed_out[len(tiles) * blocks] = rest.astype(bf16)


def score_kernel(
    own, same_core, other_core, hidden, targets, cell_node, cell_area,
    score_out, grad_out,
):
    members = 2 * same_core.shape[0]
    nodes = own.shape[1]
    variables, cells = targets.shape
    tiles, rest = lane_tiles(own[...].astype(f32))
    blocks = tiles[0].shape[0] // 16
    spreads, slopes = [], []
    for t, mine in enumerate(tiles + [rest]):
        spread = jnp.zeros_like(mine) - SMOOTH_SQ**0.5
        slope = jnp.zeros_like(mine)
        for ref in (same_core, other_core):
            for j in range(members // 2):
                if t < len(tiles):
                    other = ref[j, t * blocks : (t + 1) * blocks].reshape(mine.shape)
                else:
                    other = ref[j, t * blocks]
                delta = mine - other.astype(f32)
                square = delta * delta + SMOOTH_SQ
                inverse = lax.rsqrt(square)
                spread = spread + square * inverse
                slope = slope + delta * inverse
        spreads.append(spread)
        slopes.append(slope)
    spread = from_lane_tiles(spreads[:-1], spreads[-1])
    slope = from_lane_tiles(slopes[:-1], slopes[-1])
    kappa = ALPHA / (2.0 * members * (members - 1)) + (1.0 - ALPHA) / (2.0 * members * members)
    index = lax.broadcasted_iota(jnp.int32, (nodes, cells), 0)
    one_hot = (index == cell_node[...]).astype(bf16)
    high, low = halves(spread)
    fields = dot(own[...], one_hot)
    spread = dot(high, one_hot) + dot(low, one_hot)
    error = fields - targets[...].astype(f32)
    square = error * error + SMOOTH_SQ
    inverse = lax.rsqrt(square)
    score_out[...] = square * inverse * (1.0 / members) - kappa * spread
    area = cell_area[...]
    high, low = halves(area * (error * inverse) * (1.0 / members))
    area_high, area_low = halves(jnp.broadcast_to(area, (8, cells)))
    node_grad = dot_t(high, one_hot) + dot_t(low, one_hot)
    node_area = dot_t(area_high, one_hot) + dot_t(area_low, one_hot)
    node_grad = node_grad - (2.0 * kappa) * slope * node_area[:1]
    grad = dot(node_grad.astype(bf16), hidden[...])
    tiles = grad.shape[1] // LANES
    each = grad_out.shape[1] // 16
    grad = jnp.concatenate([grad, jnp.zeros((128 - variables, grad.shape[1]), f32)], 0).astype(bf16)
    for r in range(128 // 16):
        for c in range(tiles):
            tile = r * tiles + c
            grad_out[tile // each, pl.ds(tile % each * 16, 16), :] = grad[
                r * 16 : r * 16 + 16, c * LANES : (c + 1) * LANES
            ]


def shifted(value, axis, steps):
    count = lax.axis_size(axis)
    return lax.ppermute(value, axis, [(i, (i + steps) % count) for i in range(count)])


def copies_for(x, axis):
    return jnp.broadcast_to(x[None], (lax.axis_size(axis),) + x.shape)


def gathered(x, axis):
    return lax.all_to_all(copies_for(x, axis), axis, 0, 0)


def total(pieces):
    piece = jnp.sum(lax.all_to_all(pieces, PLANE, 0, 0).astype(f32), 0)
    piece = jnp.sum(gathered(piece.astype(bf16), LINE).astype(f32), 0)
    return gathered(piece.astype(bf16), PLANE).astype(f32)


def body(
    node_feats, norm_gain, w_query, w_key, w_value, w_out, head_scale, w_dec, targets, cell_node, cell_area
):
    feats = node_feats[0]
    nodes, width = feats.shape
    ext = nodes + 2 * HALF
    shards = lax.axis_size(GRID)
    core = lax.axis_index("core")
    variables = w_dec.shape[0]
    up = [(i, i + 1) for i in range(shards - 1)]
    before = lax.ppermute(feats[nodes - HALF :], GRID, up)
    after = lax.ppermute(feats[:HALF], GRID, [(j, i) for i, j in up])

    mine = width // 2
    rows = w_query.shape[0]
    parts = [
        lax.dynamic_slice_in_dim(w, core * mine, mine, 1) for w in (w_query, w_key, w_value, w_out)
    ]
    by_pair = jnp.stack([w.reshape(rows, mine // LANES, LANES) for w in parts[:3]], 2)
    shard = jnp.concatenate([by_pair.reshape(rows, 3 * mine), parts[3]], 1)
    lane = gathered(shard, "z_lo")
    plane = gathered(lane, "x")
    late = mine // LANES - EARLY
    cut = EARLY * 3 * LANES
    early_mine = gathered(plane[..., :cut], "y")
    early_mine, before, after, plane_late = lax.optimization_barrier(
        (early_mine, before, after, copies_for(plane[..., cut:], "y"))
    )
    late_mine = lax.all_to_all(plane_late, "y", 0, 0)
    early_other = shifted(early_mine, "core", 1)

    scale = jnp.repeat(head_scale, width // head_scale.shape[0])[None]
    edge = jnp.stack([lax.axis_index(GRID), jnp.int32(shards), core]).astype(jnp.int32)
    smem = pl.BlockSpec(memory_space=pltpu.SMEM)
    vmem = pl.BlockSpec(memory_space=pltpu.VMEM)
    anywhere = pl.BlockSpec(memory_space=pl.ANY)
    params = pltpu.CompilerParams(vmem_limit_bytes=28 * MIB)
    groups = shards // lax.axis_size("x")
    weights = lambda n: pltpu.VMEM((groups, shards // groups, rows, n), bf16)
    sem, sems = pltpu.SemaphoreType.DMA, pltpu.SemaphoreType.DMA((groups,))
    extended = pltpu.VMEM((ext, width), bf16)
    heads = lambda n: [pltpu.VMEM((2, k, n * LANES), bf16) for k in (nodes, ext, ext)]
    whole = jax.ShapeDtypeStruct((nodes, width), bf16)
    attended, normed = pl.pallas_call(
        early_kernel,
        out_shape=(whole, jax.ShapeDtypeStruct((ext, width), bf16)),
        in_specs=[smem] + [vmem] * 4 + [anywhere, anywhere, vmem],
        out_specs=(vmem, anywhere),
        scratch_shapes=[extended, weights(cut), weights(cut), *heads(EARLY), sems, sems, sem],
        compiler_params=params,
        cost_estimate=pl.CostEstimate(flops=8_000_000_000, bytes_accessed=16_000_000, transcendentals=0),
        name="early_heads",
    )(edge, before, feats, after, norm_gain[None], early_mine, early_other, scale)
    late_mine, attended = lax.optimization_barrier((late_mine, attended))
    late_other = shifted(late_mine, "core", 1)
    hidden, fields, packed = pl.pallas_call(
        late_kernel,
        out_shape=(
            whole,
            jax.ShapeDtypeStruct((variables, nodes), bf16),
            jax.ShapeDtypeStruct((variables * nodes // (16 * LANES), 16, LANES), bf16),
        ),
        in_specs=[smem, vmem, anywhere, vmem, anywhere, anywhere, vmem, vmem],
        out_specs=(vmem, vmem, vmem),
        scratch_shapes=[
            extended,
            pltpu.VMEM((nodes, width), bf16),
            weights(late * 3 * LANES),
            weights(late * 3 * LANES),
            weights(mine),
            weights(mine),
            *heads(late),
            sem,
            sems,
            sems,
            sems,
            sems,
        ],
        compiler_params=params,
        name="late_heads",
    )(edge, feats, normed, attended, late_mine, late_other, scale, w_dec)

    same_core = gathered(packed, "z_hi")
    other_core = shifted(same_core, "core", 1)
    pieces = lax.axis_size(PLANE)
    score, grad = pl.pallas_call(
        score_kernel,
        out_shape=(
            jax.ShapeDtypeStruct(targets.shape, f32),
            jax.ShapeDtypeStruct((pieces, width // pieces, LANES), bf16),
        ),
        in_specs=[vmem] * 7,
        out_specs=(vmem, vmem),
        compiler_params=params,
        name="score",
    )(fields, same_core, other_core, hidden, targets, cell_node[None], cell_area[None])
    grad = total(grad).reshape(8, width // LANES, 16, LANES).transpose(0, 2, 1, 3)
    return score[None], grad.reshape(128, width)[:variables]


def solution(mesh):
    fine = Mesh(mesh.devices.reshape(4, 2, 4, 4, 4), MEMBER + GRID)
    in_specs = (
        P(MEMBER, GRID, None),
        P(),
        P(GRID, None),
        P(GRID, None),
        P(GRID, None),
        P(GRID, None),
        P(),
        P(),
        P(None, GRID),
        P(GRID),
        P(GRID),
    )
    out_specs = (P(MEMBER, None, GRID), P())
    return jax.shard_map(body, mesh=fine, in_specs=in_specs, out_specs=out_specs, check_vma=False)
```

```python
import functools

import jax
import jax.numpy as jnp
from jax import lax
from jax.experimental import pallas as pl
from jax.experimental.pallas import tpu as pltpu
from jax.sharding import Mesh, PartitionSpec as P

HALF = 256
EPS = 1e-06
SMOOTH_SQ = 0.0625
ALPHA = 0.95
LANES = 128
BLOCK = 128
LOW = -1e30
MIB = 1024 * 1024
EARLY = 3
SKEW = 2

GRID = ("y", "z_lo", "x")
MEMBER = ("z_hi", "core")
PLANE = ("core", "y", "x")
LINE = ("z_hi", "z_lo")

f32 = jnp.float32
bf16 = jnp.bfloat16


def dot(a, b):
    return jnp.dot(a, b, preferred_element_type=f32)


def dot_t(a, b):
    return lax.dot_general(a, b, (((1,), (1,)), ((), ())), preferred_element_type=f32)


def halves(x):
    high = x.astype(bf16)
    return high, (x - high.astype(f32)).astype(bf16)


def loop(count, fn):
    def step(i, _):
        fn(i)
        return 0

    lax.fori_loop(0, count, step, 0)


def normalise(before, feats, after, gain, normed):
    gain_row = gain[...].astype(f32)
    start = 0
    for ref in (before, feats, after):

        def norm(i, ref=ref, start=start):
            x = ref[pl.ds(pl.multiple_of(i * 64, 64), 64), :].astype(f32)
            mean = jnp.mean(x * x, -1, keepdims=True)
            y = x * lax.rsqrt(mean + EPS) * gain_row
            normed[pl.ds(pl.multiple_of(start + i * 64, 64), 64), :] = y.astype(bf16)

        loop(ref.shape[0] // 64, norm)
        start += ref.shape[0]


def lane_tiles(x):
    whole = x.shape[0] // 16 * 16
    tiles = [x[:, t * LANES : (t + 1) * LANES] for t in range(x.shape[1] // LANES)]
    return [tile[:whole] for tile in tiles], jnp.concatenate([tile[whole:] for tile in tiles], 0)


def from_lane_tiles(tiles, rest):
    each = rest.shape[0] // len(tiles)
    whole = [
        jnp.concatenate([tile, rest[t * each : (t + 1) * each]], 0) for t, tile in enumerate(tiles)
    ]
    return jnp.concatenate(whole, 1)


def weight_copies(gathered_weights, weights, sems):
    ys, xs, zs, rows, _ = gathered_weights.shape
    copies = []
    for y in range(ys):
        for z in range(zs):
            copies.append(
                pltpu.make_async_copy(
                    gathered_weights.at[y, :, z], weights.at[y * zs + z], sems.at[y * zs + z]
                )
            )
    return copies


def attend_pairs(edge, normed, weights, scale, half, first, query, keys, values, attended):
    base = half * (scale.shape[1] // 2) + first * LANES
    ext, width = normed.shape
    nodes = ext - 2 * HALF
    pairs = weights.shape[-1] // (3 * LANES)
    flat = weights.reshape(width, weights.shape[-1])

    def unit(y):
        first_head = lax.broadcasted_iota(jnp.int32, y.shape, 1) < 64
        square = y * y
        first = jnp.sum(jnp.where(first_head, square, 0.0), -1, keepdims=True)
        second = jnp.sum(jnp.where(first_head, 0.0, square), -1, keepdims=True)
        return y * lax.rsqrt(jnp.where(first_head, first, second) + EPS)

    def project(p):
        cols = pl.ds(p * LANES, LANES)
        query_cols = pl.ds(p * 3 * LANES, LANES)
        keyval_cols = pl.ds(p * 3 * LANES + LANES, 2 * LANES)
        factor = scale[:, pl.ds(pl.multiple_of(base + p * LANES, LANES), LANES)]
        for r in range(nodes // 256):
            rows = pl.ds(r * 256, 256)
            y = dot(normed[pl.ds(HALF + r * 256, 256), :], flat[:, query_cols])
            query[rows, cols] = (unit(y) * factor).astype(bf16)
        for r in range(ext // 256):
            rows = pl.ds(r * 256, 256)
            y = dot(normed[rows, :], flat[:, keyval_cols])
            keys[rows, cols] = unit(y[:, :LANES]).astype(bf16)
            values[rows, cols] = y[:, LANES:].astype(bf16)

    row = lax.broadcasted_iota(jnp.int32, (2 * BLOCK, BLOCK), 0) % BLOCK
    col = lax.broadcasted_iota(jnp.int32, (2 * BLOCK, BLOCK), 1)
    lead = jnp.where(col >= row, 0.0, LOW).astype(f32)
    tail = jnp.where(col < row, 0.0, LOW).astype(f32)
    first_head = lax.broadcasted_iota(jnp.int32, (BLOCK, LANES), 1) < 64
    ones = jnp.ones((2 * HALF + BLOCK, LANES), bf16)
    segments = 2 * HALF // BLOCK + 1
    blocks = nodes // BLOCK
    out_low = jnp.where(edge[0] == 0, LOW, 0.0).astype(f32)
    out_high = jnp.where(edge[0] == edge[1] - 1, LOW, 0.0).astype(f32)

    def scores(p, b):
        cols = pl.ds(p * LANES, LANES)
        q = query[pl.ds(b * BLOCK, BLOCK), cols]
        zero = jnp.zeros_like(q)
        pair = jnp.concatenate([jnp.where(first_head, q, zero), jnp.where(first_head, zero, q)], 0)
        score = dot_t(pair, keys[pl.ds(b * BLOCK, 2 * HALF + BLOCK), cols])
        parts = []
        for s in range(segments):
            part = score[:, s * BLOCK : (s + 1) * BLOCK]
            if s == 0:
                part = part + lead
            if s == segments - 1:
                part = part + tail
            if (b + s + 1) * BLOCK <= HALF:
                part = part + out_low
            if (b + s) * BLOCK >= HALF + nodes:
                part = part + out_high
            parts.append(part)
        return parts

    def softened(parts):
        top = functools.reduce(jnp.maximum, parts)
        top = jnp.max(top, -1, keepdims=True)
        return jnp.concatenate([jnp.exp(part - top).astype(bf16) for part in parts], 1)

    def mix(p, b, weight):
        window = pl.ds(b * BLOCK, 2 * HALF + BLOCK)
        value = values[window, pl.ds(p * LANES, LANES)]
        mixed = dot(weight, jnp.concatenate([value, ones], 1))
        mixed = mixed[:, :LANES] / mixed[:, LANES:]
        out_cols = pl.ds(pl.multiple_of(base + p * LANES, LANES), LANES)
        attended[pl.ds(b * BLOCK, BLOCK), out_cols] = jnp.where(
            first_head, mixed[:BLOCK], mixed[BLOCK:]
        ).astype(bf16)

    items = [(p, b) for p in range(pairs) for b in range(blocks)]
    score, weight = {}, {}
    project(0)
    for i in range(len(items) + 2 * SKEW):
        if i < len(items):
            if i % blocks == 0 and i // blocks + 1 < pairs:
                project(i // blocks + 1)
            score[i] = scores(*items[i])
        j = i - SKEW
        if 0 <= j < len(items):
            weight[j] = softened(score.pop(j))
        k = j - SKEW
        if 0 <= k < len(items):
            mix(*items[k], weight.pop(k))


def early_kernel(
    edge, before, feats, after, gain, gathered_mine, gathered_other, scale,
    attended, normed_out,
    normed, weights_mine, weights_other, query, keys, values, sems_mine, sems_other, out_sem,
):
    copies_mine = weight_copies(gathered_mine, weights_mine, sems_mine)
    copies_other = weight_copies(gathered_other, weights_other, sems_other)
    for copy in copies_mine + copies_other:
        copy.start()
    normalise(before, feats, after, gain, normed)
    leave = pltpu.make_async_copy(normed, normed_out, out_sem)
    leave.start()
    for i, (half, weights, copies) in enumerate(
        ((edge[2], weights_mine, copies_mine), (1 - edge[2], weights_other, copies_other))
    ):
        for copy in copies:
            copy.wait()
        attend_pairs(edge, normed, weights, scale, half, 0, query.at[i], keys.at[i], values.at[i], attended)
    leave.wait()


def late_kernel(
    edge, feats, normed_in, attended_early, gathered_mine, gathered_other, scale, w_dec,
    hidden_out, fields_out, packed_out,
    normed, attended, weights_mine, weights_other, out_mine, out_other, query, keys, values,
    in_sem, sems_mine, sems_other, sems_out_mine, sems_out_other,
):
    nodes, width = feats.shape
    mine = width // 2
    columns = weights_mine.shape[-1]
    heads, out = pl.ds(0, columns), pl.ds(columns, mine)
    enter = pltpu.make_async_copy(normed_in, normed, in_sem)
    copies_mine = weight_copies(gathered_mine.at[..., heads], weights_mine, sems_mine)
    copies_other = weight_copies(gathered_other.at[..., heads], weights_other, sems_other)
    copies_out = weight_copies(gathered_mine.at[..., out], out_mine, sems_out_mine)
    copies_out += weight_copies(gathered_other.at[..., out], out_other, sems_out_other)
    for copy in [enter] + copies_mine + copies_other + copies_out:
        copy.start()
    attended[...] = attended_early[...]
    enter.wait()
    for i, (half, weights, copies) in enumerate(
        ((edge[2], weights_mine, copies_mine), (1 - edge[2], weights_other, copies_other))
    ):
        for copy in copies:
            copy.wait()
        attend_pairs(edge, normed, weights, scale, half, EARLY, query.at[i], keys.at[i], values.at[i], attended)
    here = pl.ds(pl.multiple_of(edge[2] * mine, mine), mine)
    there = pl.ds(pl.multiple_of((1 - edge[2]) * mine, mine), mine)
    for copy in copies_out:
        copy.wait()
    for half, cols in ((out_mine, here), (out_other, there)):
        flat = half.reshape(width, mine)
        for r in range(nodes // 256):
            rows = pl.ds(r * 256, 256)
            hidden = feats[rows, cols].astype(f32) + dot(attended[rows, :], flat[...])
            hidden_out[rows, cols] = hidden.astype(bf16)
    fields = dot_t(w_dec[...], hidden_out[...])
    fields_out[...] = fields.astype(bf16)
    tiles, rest = lane_tiles(fields)
    blocks = tiles[0].shape[0] // 16
    for t, tile in enumerate(tiles):
        for i in range(blocks):
            packed_out[t * blocks + i] = tile[i * 16 : i * 16 + 16].astype(bf16)
    packed_out[len(tiles) * blocks] = rest.astype(bf16)


def one_hot_cells(cell_node, nodes):
    index = lax.broadcasted_iota(jnp.int32, (nodes, cell_node.shape[1]), 0)
    return (index == cell_node[...]).astype(bf16)


def error_kernel(members, own, targets, cell_node, cell_area, error_out, node_out, area_out):
    one_hot = one_hot_cells(cell_node, own.shape[1])
    fields = dot(own[...], one_hot)
    error = fields - targets[...].astype(f32)
    square = error * error + SMOOTH_SQ
    inverse = lax.rsqrt(square)
    error_out[...] = square * inverse * (1.0 / members)
    area = cell_area[...]
    high, low = halves(area * (error * inverse) * (1.0 / members))
    area_high, area_low = halves(jnp.broadcast_to(area, area_out.shape[:1] + area.shape[1:]))
    node_out[...] = dot_t(high, one_hot) + dot_t(low, one_hot)
    area_out[...] = dot_t(area_high, one_hot) + dot_t(area_low, one_hot)


def score_kernel(
    own, same_core, other_core, hidden, cell_node, error_part, node_part, node_area,
    score_out, grad_out,
):
    members = 2 * same_core.shape[0]
    variables, nodes = own.shape
    tiles, rest = lane_tiles(own[...].astype(f32))
    blocks = tiles[0].shape[0] // 16
    spreads, slopes = [], []
    for t, mine in enumerate(tiles + [rest]):
        spread = jnp.zeros_like(mine) - SMOOTH_SQ**0.5
        slope = jnp.zeros_like(mine)
        for ref in (same_core, other_core):
            for j in range(members // 2):
                if t < len(tiles):
                    other = ref[j, t * blocks : (t + 1) * blocks].reshape(mine.shape)
                else:
                    other = ref[j, t * blocks]
                delta = mine - other.astype(f32)
                square = delta * delta + SMOOTH_SQ
                inverse = lax.rsqrt(square)
                spread = spread + square * inverse
                slope = slope + delta * inverse
        spreads.append(spread)
        slopes.append(slope)
    spread = from_lane_tiles(spreads[:-1], spreads[-1])
    slope = from_lane_tiles(slopes[:-1], slopes[-1])
    kappa = ALPHA / (2.0 * members * (members - 1)) + (1.0 - ALPHA) / (2.0 * members * members)
    one_hot = one_hot_cells(cell_node, nodes)
    high, low = halves(spread)
    spread = dot(high, one_hot) + dot(low, one_hot)
    score_out[...] = error_part[...] - kappa * spread
    node_grad = node_part[...] - (2.0 * kappa) * slope * node_area[:1, :]
    grad = dot(node_grad.astype(bf16), hidden[...])
    tiles = grad.shape[1] // LANES
    each = grad_out.shape[1] // 16
    grad = jnp.concatenate([grad, jnp.zeros((128 - variables, grad.shape[1]), f32)], 0).astype(bf16)
    for r in range(128 // 16):
        for c in range(tiles):
            tile = r * tiles + c
            grad_out[tile // each, pl.ds(tile % each * 16, 16), :] = grad[
                r * 16 : r * 16 + 16, c * LANES : (c + 1) * LANES
            ]


def shifted(value, axis, steps):
    count = lax.axis_size(axis)
    return lax.ppermute(value, axis, [(i, (i + steps) % count) for i in range(count)])


def copies_for(x, axis):
    return jnp.broadcast_to(x[None], (lax.axis_size(axis),) + x.shape)


def gathered(x, axis):
    return lax.all_to_all(copies_for(x, axis), axis, 0, 0)


def total(pieces):
    piece = jnp.sum(lax.all_to_all(pieces, PLANE, 0, 0).astype(f32), 0)
    piece = jnp.sum(gathered(piece.astype(bf16), LINE).astype(f32), 0)
    return gathered(piece.astype(bf16), PLANE).astype(f32)


def body(
    node_feats, norm_gain, w_query, w_key, w_value, w_out, head_scale, w_dec, targets, cell_node, cell_area
):
    feats = node_feats[0]
    nodes, width = feats.shape
    ext = nodes + 2 * HALF
    shards = lax.axis_size(GRID)
    core = lax.axis_index("core")
    variables = w_dec.shape[0]
    up = [(i, i + 1) for i in range(shards - 1)]
    before = lax.ppermute(feats[nodes - HALF :], GRID, up)
    after = lax.ppermute(feats[:HALF], GRID, [(j, i) for i, j in up])

    mine = width // 2
    rows = w_query.shape[0]
    parts = [
        lax.dynamic_slice_in_dim(w, core * mine, mine, 1) for w in (w_query, w_key, w_value, w_out)
    ]
    by_pair = jnp.stack([w.reshape(rows, mine // LANES, LANES) for w in parts[:3]], 2)
    shard = jnp.concatenate([by_pair.reshape(rows, 3 * mine), parts[3]], 1)
    lane = gathered(shard, "z_lo")
    plane = gathered(lane, "x")
    late = mine // LANES - EARLY
    cut = EARLY * 3 * LANES
    early_mine = gathered(plane[..., :cut], "y")
    early_mine, before, after, plane_late = lax.optimization_barrier(
        (early_mine, before, after, copies_for(plane[..., cut:], "y"))
    )
    late_mine = lax.all_to_all(plane_late, "y", 0, 0)
    early_other = shifted(early_mine, "core", 1)

    scale = jnp.repeat(head_scale, width // head_scale.shape[0])[None]
    edge = jnp.stack([lax.axis_index(GRID), jnp.int32(shards), core]).astype(jnp.int32)
    smem = pl.BlockSpec(memory_space=pltpu.SMEM)
    vmem = pl.BlockSpec(memory_space=pltpu.VMEM)
    anywhere = pl.BlockSpec(memory_space=pl.ANY)
    params = pltpu.CompilerParams(vmem_limit_bytes=28 * MIB)
    groups = shards // lax.axis_size("x")
    weights = lambda n: pltpu.VMEM((groups, shards // groups, rows, n), bf16)
    sem, sems = pltpu.SemaphoreType.DMA, pltpu.SemaphoreType.DMA((groups,))
    extended = pltpu.VMEM((ext, width), bf16)
    heads = lambda n: [pltpu.VMEM((2, k, n * LANES), bf16) for k in (nodes, ext, ext)]
    whole = jax.ShapeDtypeStruct((nodes, width), bf16)
    attended, normed = pl.pallas_call(
        early_kernel,
        out_shape=(whole, jax.ShapeDtypeStruct((ext, width), bf16)),
        in_specs=[smem] + [vmem] * 4 + [anywhere, anywhere, vmem],
        out_specs=(vmem, anywhere),
        scratch_shapes=[extended, weights(cut), weights(cut), *heads(EARLY), sems, sems, sem],
        compiler_params=params,
        cost_estimate=pl.CostEstimate(flops=8_000_000_000, bytes_accessed=16_000_000, transcendentals=0),
        name="early_heads",
    )(edge, before, feats, after, norm_gain[None], early_mine, early_other, scale)
    late_mine, attended = lax.optimization_barrier((late_mine, attended))
    late_other = shifted(late_mine, "core", 1)
    hidden, fields, packed = pl.pallas_call(
        late_kernel,
        out_shape=(
            whole,
            jax.ShapeDtypeStruct((variables, nodes), bf16),
            jax.ShapeDtypeStruct((variables * nodes // (16 * LANES), 16, LANES), bf16),
        ),
        in_specs=[smem, vmem, anywhere, vmem, anywhere, anywhere, vmem, vmem],
        out_specs=(vmem, vmem, vmem),
        scratch_shapes=[
            extended,
            pltpu.VMEM((nodes, width), bf16),
            weights(late * 3 * LANES),
            weights(late * 3 * LANES),
            weights(mine),
            weights(mine),
            *heads(late),
            sem,
            sems,
            sems,
            sems,
            sems,
        ],
        compiler_params=params,
        name="late_heads",
    )(edge, feats, normed, attended, late_mine, late_other, scale, w_dec)

    members = lax.axis_size(MEMBER)
    error_part, node_part, node_area = pl.pallas_call(
        functools.partial(error_kernel, members),
        out_shape=(
            jax.ShapeDtypeStruct(targets.shape, f32),
            jax.ShapeDtypeStruct((variables, nodes), f32),
            jax.ShapeDtypeStruct((8, nodes), f32),
        ),
        in_specs=[vmem] * 4,
        out_specs=(vmem, vmem, vmem),
        compiler_params=params,
        name="error",
    )(fields, targets, cell_node[None], cell_area[None])
    same_core = gathered(packed, "z_hi")
    other_core = shifted(same_core, "core", 1)
    pieces = lax.axis_size(PLANE)
    score, grad = pl.pallas_call(
        score_kernel,
        out_shape=(
            jax.ShapeDtypeStruct(targets.shape, f32),
            jax.ShapeDtypeStruct((pieces, width // pieces, LANES), bf16),
        ),
        in_specs=[vmem] * 8,
        out_specs=(vmem, vmem),
        compiler_params=params,
        name="score",
    )(fields, same_core, other_core, hidden, cell_node[None], error_part, node_part, node_area)
    grad = total(grad).reshape(8, width // LANES, 16, LANES).transpose(0, 2, 1, 3)
    return score[None], grad.reshape(128, width)[:variables]


def solution(mesh):
    fine = Mesh(mesh.devices.reshape(4, 2, 4, 4, 4), MEMBER + GRID)
    in_specs = (
        P(MEMBER, GRID, None),
        P(),
        P(GRID, None),
        P(GRID, None),
        P(GRID, None),
        P(GRID, None),
        P(),
        P(),
        P(None, GRID),
        P(GRID),
        P(GRID),
    )
    out_specs = (P(MEMBER, None, GRID), P())
    return jax.shard_map(body, mesh=fine, in_specs=in_specs, out_specs=out_specs, check_vma=False)
```
